512 devices in a mesh: node: 32 (over x, y, core), local: 16 (over z).
Axes of the slice: x: 4, y: 4, z: 16, core: 2. Of those that a mesh axis runs over, the one named last changes fastest.
Arguments:
- tokens: bfloat16 [2048, 6144], P('node', 'local'), may hold values from -6 to 6
- cotangent: bfloat16 [2048, 6144], P('node', 'local'), may hold values from -6 to 6
- node_list: int32 [2048, 4], P('node'), may hold values from 0 to 31, as said below
- expert_ids: int32 [2048, 6], P('node'), may hold values from 0 to 63, as said below
- gate_ints: int32 [2048, 6], P('node'), may hold values from 1 to 1023
- w_gate: bfloat16 [6144, 65536], P(None, ('node', 'local')), may hold values from -0.078125 to 0.078125
- w_up: bfloat16 [6144, 65536], P(None, ('node', 'local')), may hold values from -0.078125 to 0.078125
- w_down: bfloat16 [65536, 6144], P('node', 'local'), may hold values from -0.1875 to 0.1875
Outputs:
- mixed: bfloat16 [2048, 6144], P('node', 'local')
- grad_tokens: bfloat16 [2048, 6144], P('node', 'local')
The draws below stay inside these ranges and needn't reach their ends.
Inputs may be any that keep to these rules, and one draw needn't show every extreme that they name: `node_list`: A token's 4 node groups are distinct; the tokens of each node group name every node group exactly 8 times in all. `expert_ids`: A token's 6 experts are distinct, and each lies in one of the token's node groups (expert e lies in group e // 2).
All inputs are finite; a program needn't handle non-finite values.
Results may differ from the reference program's by a relative error of at most 0.034.
Values may be sent and summed in bfloat16 or wider, within the bound.
No kernel may reach another device: no remote copies, remote signals or barrier semaphores. Data moves between devices by JAX's collectives and lax.ppermute only.
A program may use at most 64 MiB of HBM per device.

```python
import jax
import jax.numpy as jnp
from jax import lax

D = 6144
FF = 1024
EXP_NODE = 2
NODES_TOK = 4
TOPK = 6
TOK_NODE = 64
TOKENS = 2048
EXPERTS = 64
FEAT = 384
H_DEV = 128
ROWS = 256
CAP = 8
N_NODE = 32
N_LOCAL = 16


def routing(key):
    token_keys = jax.random.split(jax.random.fold_in(key, 11), N_NODE)
    node_keys = jax.random.split(jax.random.fold_in(key, 12), N_NODE)
    token_order = jax.vmap(lambda sub_key: jax.random.permutation(sub_key, TOK_NODE))(token_keys)
    node_order = jax.vmap(lambda sub_key: jax.random.permutation(sub_key, N_NODE))(node_keys)
    places = (token_order[:, :, None] * NODES_TOK + jnp.arange(NODES_TOK)[None, None, :]) % N_NODE
    chosen = jnp.take_along_axis(node_order, places.reshape(N_NODE, TOK_NODE * NODES_TOK), axis=1)
    return chosen.reshape(TOKENS, NODES_TOK).astype(jnp.int32)


def draw_node_list(key, part):
    chosen = routing(key)
    return chosen


def draw_expert_ids(key, part):
    chosen = routing(key)
    key = jax.random.fold_in(key, 2)
    slots_all = NODES_TOK * EXP_NODE
    column = jnp.arange(slots_all, dtype=jnp.int32)
    scores = jax.random.randint(key, (TOKENS, slots_all), 0, 16) + 6 * (column % EXP_NODE)[None, :]
    order = jnp.argsort(scores * slots_all + column[None, :], axis=1)[:, :TOPK]
    experts = jnp.take_along_axis(chosen, order // EXP_NODE, axis=1) * EXP_NODE + order % EXP_NODE
    return experts.astype(jnp.int32)


def with_ends(array, stream_key, low, largest):
    place = [jax.random.randint(jax.random.fold_in(stream_key, axis), (), 0, length) for axis, length in enumerate(array.shape)]
    main_axis = array.shape.index(max(array.shape))
    next_to = place[:main_axis] + [(place[main_axis] + 1) % array.shape[main_axis]] + place[main_axis + 1:]
    return array.at[tuple(place)].set(low).at[tuple(next_to)].set(largest)


def levels(rng, shape, shards, low, high):
    loudness, own = 1.0, jax.random.fold_in(rng, 6)
    for dim, shards_of in shards:
        draws = jnp.exp(jax.random.uniform(jax.random.fold_in(own, dim), (shards_of,), jnp.float32, low / len(shards), high / len(shards)))
        loudness = loudness * jnp.repeat(draws, shape[dim] // shards_of).reshape([-1 if axis == dim else 1 for axis in range(len(shape))])
    return loudness


def normal_values(rng, dims, spread, most, cuts=(), kind=jnp.bfloat16):
    drawn = spread * jax.random.normal(rng, dims, jnp.float32)
    if cuts:
        drawn = drawn * levels(rng, dims, cuts, -0.22, 0.18)
    return jnp.clip(drawn, -most, most).astype(kind)


def setup_inputs(seed: int = 0) -> dict:
    key_of = jax.random.split(jax.random.key(seed), 9)
    tokens = normal_values(key_of[0], (TOKENS, D), 1.0, 6.0, ((0, 32), (1, 16)))
    cotangent = normal_values(key_of[1], (TOKENS, D), 1.0, 6.0, ((0, 32), (1, 16)))
    node_list = draw_node_list(jax.random.fold_in(key_of[8], 71), 0)
    expert_ids = draw_expert_ids(jax.random.fold_in(key_of[8], 71), 0)
    gate_ints = with_ends(jax.random.randint(key_of[4], (TOKENS, TOPK), 1, 1024), jax.random.fold_in(key_of[4], 1), 1, 1023).astype(jnp.int32)
    w_gate = normal_values(key_of[5], (D, EXPERTS * FF), D ** -0.5, 0.078125, ((1, 512),))
    w_up = normal_values(key_of[6], (D, EXPERTS * FF), D ** -0.5, 0.078125, ((1, 512),))
    w_down = normal_values(key_of[7], (EXPERTS * FF, D), FF ** -0.5, 0.1875, ((0, 32), (1, 16)))
    return dict(tokens=tokens, cotangent=cotangent, node_list=node_list, expert_ids=expert_ids, gate_ints=gate_ints, w_gate=w_gate, w_up=w_up, w_down=w_down)


def routing_gates(node_list, expert_ids, gate_ints):
    counts = gate_ints.astype(jnp.float32)
    weight_share = counts / jnp.sum(counts, axis=1, keepdims=True)
    within = jnp.arange(EXP_NODE, dtype=jnp.int32)
    candidate = node_list[:, :, None] * EXP_NODE + within[None, None, :]
    match_table = expert_ids[:, None, None, :] == candidate[:, :, :, None]
    picked = jnp.where(match_table, weight_share[:, None, None, :], jnp.float32(0.0))
    return jnp.sum(picked, axis=3).astype(jnp.bfloat16)


def reference(tokens, cotangent, node_list, expert_ids, gate_ints, w_gate, w_up, w_down):
    node_hidden = EXP_NODE * FF
    flat_count = TOKENS * NODES_TOK
    route_gate = routing_gates(node_list, expert_ids, gate_ints).reshape(flat_count, EXP_NODE)
    node_flat = node_list.reshape(flat_count)
    onehot = (node_flat[:, None] == jnp.arange(N_NODE, dtype=jnp.int32)[None, :]).astype(jnp.int32)
    grouped = onehot.reshape(N_NODE, TOK_NODE * NODES_TOK, N_NODE)
    before = (jnp.cumsum(grouped, axis=1) - grouped).reshape(flat_count, N_NODE)
    slot_index = jnp.sum(before * onehot, axis=1).astype(jnp.int32)
    group_index = jnp.arange(flat_count, dtype=jnp.int32) // (TOK_NODE * NODES_TOK)
    arrivals = jnp.zeros((N_NODE, ROWS), jnp.int32).at[node_flat, group_index * CAP + slot_index].set(
        jnp.arange(flat_count, dtype=jnp.int32))

    def one_node(running, node_id):
        mixed_sum, grad_sum = running
        flat_rows = arrivals[node_id]
        token_rows = flat_rows // NODES_TOK
        rows_in = tokens[token_rows]
        grads_in = cotangent[token_rows]
        gate_rows = jnp.repeat(route_gate[flat_rows].astype(jnp.float32), FF, axis=1)
        first = (node_id * node_hidden).astype(jnp.int32)
        gate_cols = lax.dynamic_slice_in_dim(w_gate, first, node_hidden, 1)
        up_cols = lax.dynamic_slice_in_dim(w_up, first, node_hidden, 1)
        down_rows = lax.dynamic_slice_in_dim(w_down, first, node_hidden, 0)
        pre_gate = jnp.dot(rows_in, gate_cols, preferred_element_type=jnp.float32)
        pre_up = jnp.dot(rows_in, up_cols, preferred_element_type=jnp.float32)
        sigmoid_gate = jax.nn.sigmoid(pre_gate)
        swish = pre_gate * sigmoid_gate
        activation = (swish * pre_up * gate_rows).astype(jnp.bfloat16)
        node_out = jnp.dot(activation, down_rows, preferred_element_type=jnp.float32)

        def act_block(block_id, accum):
            low_index = (block_id * FEAT).astype(jnp.int32)
            grad_block = lax.dynamic_slice_in_dim(grads_in, low_index, FEAT, 1)
            down_block = lax.dynamic_slice_in_dim(down_rows, low_index, FEAT, 1)
            partial_value = jnp.dot(grad_block, down_block.T, preferred_element_type=jnp.float32)
            return accum + lax.optimization_barrier(partial_value.astype(jnp.bfloat16)).astype(jnp.float32)

        grad_act = lax.fori_loop(jnp.int32(0), jnp.int32(N_LOCAL), act_block,
                                 jnp.zeros((ROWS, node_hidden), jnp.float32))
        grad_up = (grad_act * gate_rows * swish).astype(jnp.bfloat16)
        grad_pre = (grad_act * gate_rows * pre_up * sigmoid_gate
                    * (1.0 + pre_gate * (1.0 - sigmoid_gate))).astype(jnp.bfloat16)

        def input_block(block_id, accum):
            low_index = (block_id * H_DEV).astype(jnp.int32)
            pre_block = lax.dynamic_slice_in_dim(grad_pre, low_index, H_DEV, 1)
            up_block = lax.dynamic_slice_in_dim(grad_up, low_index, H_DEV, 1)
            gate_block = lax.dynamic_slice_in_dim(gate_cols, low_index, H_DEV, 1)
            upw_block = lax.dynamic_slice_in_dim(up_cols, low_index, H_DEV, 1)
            partial_value = jnp.dot(pre_block, gate_block.T, preferred_element_type=jnp.float32)
            partial_value = partial_value + jnp.dot(up_block, upw_block.T, preferred_element_type=jnp.float32)
            return accum + lax.optimization_barrier(partial_value.astype(jnp.bfloat16)).astype(jnp.float32)

        row_grad = lax.fori_loop(jnp.int32(0), jnp.int32(N_LOCAL), input_block,
                                 jnp.zeros((ROWS, D), jnp.float32))
        return (mixed_sum.at[token_rows].add(node_out), grad_sum.at[token_rows].add(row_grad)), None

    start_sums = (jnp.zeros((TOKENS, D), jnp.float32), jnp.zeros((TOKENS, D), jnp.float32))
    (mixed_sum, grad_sum), _ = lax.scan(one_node, start_sums, jnp.arange(N_NODE, dtype=jnp.int32))
    return mixed_sum.astype(jnp.bfloat16), grad_sum.astype(jnp.bfloat16)
```

```python
import functools

import jax
import jax.numpy as jnp
from jax import lax
from jax.experimental import pallas as pl
from jax.experimental.pallas import tpu as pltpu
from jax.sharding import PartitionSpec as P

EXP_NODE = 2
F32 = jnp.float32
BF16 = jnp.bfloat16
NT = (((1,), (1,)), ((), ()))
TN = (((0,), (0,)), ((), ()))
NN = (((1,), (0,)), ((), ()))


def dot(a, b, dims=NN):
    return lax.dot_general(a, b, dims, preferred_element_type=F32)


def kernel_call(body, outs, args, flops, in_specs=None):
    moved = sum(a.size * a.dtype.itemsize for a in args)
    moved += sum(o.size * o.dtype.itemsize for o in outs)
    vmem = pl.BlockSpec(memory_space=pltpu.VMEM)
    return pl.pallas_call(
        body,
        out_shape=outs,
        in_specs=in_specs or [vmem] * len(args),
        out_specs=[vmem] * len(outs),
        compiler_params=pltpu.CompilerParams(vmem_limit_bytes=32 * 1024 * 1024),
        cost_estimate=pl.CostEstimate(flops=flops, bytes_accessed=moved, transcendentals=0),
    )(*args)


def shape(dims, dtype=BF16):
    return jax.ShapeDtypeStruct(dims, dtype)


def route_body(cap, own_ref, nodes_ref, experts_ref, counts_ref, cot_ref, place_ref, send_ref):
    slots, toks = place_ref.shape
    feat = cot_ref.shape[1]
    slot = lax.broadcasted_iota(jnp.int32, (slots, toks), 0)
    group = slot // cap
    within = slot - group * cap
    named = jnp.zeros((slots, toks), F32)
    for j in range(nodes_ref.shape[0]):
        named = jnp.where(nodes_ref[j : j + 1, :] == group, 1.0, named)
    before = lax.broadcasted_iota(jnp.int32, (toks, toks), 0)
    after = lax.broadcasted_iota(jnp.int32, (toks, toks), 1)
    earlier = jnp.where(before < after, 1.0, 0.0).astype(BF16)
    rank = dot(named.astype(BF16), earlier)
    place = jnp.where(rank == within.astype(F32), named, 0.0)
    place_ref[...] = place.astype(BF16)
    counts = counts_ref[...].astype(F32)
    share = counts / jnp.sum(counts, axis=0, keepdims=True)
    expert = group * EXP_NODE + own_ref[0]
    picked = jnp.zeros((slots, toks), F32)
    for k in range(experts_ref.shape[0]):
        picked = picked + jnp.where(experts_ref[k : k + 1, :] == expert, share[k : k + 1, :], 0.0)
    gate = jnp.sum(picked * place, axis=1, keepdims=True)
    send_ref[:, :feat] = dot(place.astype(BF16), cot_ref[...]).astype(BF16)
    send_ref[:, feat:] = jnp.broadcast_to(gate, (slots, send_ref.shape[1] - feat)).astype(BF16)


def spread_body(order, feat, place_ref, full_ref, send_ref):
    for index, z in enumerate(order):
        rows = dot(place_ref[...], full_ref[index])
        send_ref[:, z * feat : (z + 1) * feat] = rows.astype(BF16)


def act_grad_body(feat, got_ref, down_ref, out_ref):
    hidden = out_ref.shape[2]
    for z in range(out_ref.shape[0]):
        out_ref[z] = dot(got_ref[:, :feat], down_ref[z * hidden : (z + 1) * hidden, :], NT).astype(BF16)


def up_body(feat, rows_ref, gate_w_ref, up_w_ref, got_ref, act_ref, pre_gate_ref, pre_up_ref):
    pre_gate = dot(rows_ref[...], gate_w_ref[...])
    pre_up = dot(rows_ref[...], up_w_ref[...])
    gate = got_ref[:, feat:].astype(F32)
    act_ref[...] = (pre_gate * jax.nn.sigmoid(pre_gate) * pre_up * gate).astype(BF16)
    pre_gate_ref[...] = pre_gate
    pre_up_ref[...] = pre_up


def row_grad_body(feat, grad_ref, pre_gate_ref, pre_up_ref, got_ref, gate_w_ref, up_w_ref, out_ref):
    pre_gate = pre_gate_ref[...]
    sig = jax.nn.sigmoid(pre_gate)
    scaled = grad_ref[...].astype(F32) * got_ref[:, feat:].astype(F32)
    grad_up = (scaled * (pre_gate * sig)).astype(BF16)
    grad_pre = (scaled * pre_up_ref[...] * sig * (1.0 + pre_gate * (1.0 - sig))).astype(BF16)
    for z in range(out_ref.shape[0]):
        cols = slice(z * feat, (z + 1) * feat)
        part = dot(grad_pre, gate_w_ref[cols, :], NT) + dot(grad_up, up_w_ref[cols, :], NT)
        out_ref[z] = part.astype(BF16)


def down_body(order, act_ref, down_ref, out_ref):
    hidden = act_ref.shape[2]
    total = jnp.zeros(out_ref.shape, F32)
    for index, z in enumerate(order):
        total = total + dot(act_ref[index], down_ref[z * hidden : (z + 1) * hidden, :])
    out_ref[...] = total.astype(BF16)


def combine_body(place_ref, back_ref, out_ref):
    out_ref[...] = dot(place_ref[...], back_ref[...], TN).astype(BF16)


def per_device(tokens, cotangent, node_list, expert_ids, gate_ints, w_gate, w_up, w_down):
    toks, feat = tokens.shape
    width, hidden = w_gate.shape
    nodes = lax.axis_size("node")
    local = lax.axis_size("local")
    slots = toks * node_list.shape[1]
    cap = slots // nodes
    low = 4
    high = local // low
    far_groups = [[low * b + a for b in range(high)] for a in range(low)]
    near_groups = [[low * a + b for b in range(low)] for a in range(high)]
    order = [low * b + a for a in range(low) for b in range(high)]
    extra = 128

    def swap_nodes(value):
        cut = value.reshape(nodes, cap, value.shape[1])
        moved = lax.all_to_all(cut, "node", split_axis=0, concat_axis=0, tiled=True)
        return moved.reshape(value.shape)

    own = (lax.axis_index("local") // (local // EXP_NODE)).astype(jnp.int32).reshape(1)
    smem = pl.BlockSpec(memory_space=pltpu.SMEM)
    vmem = pl.BlockSpec(memory_space=pltpu.VMEM)
    place, send = kernel_call(
        functools.partial(route_body, cap),
        [shape((slots, toks)), shape((slots, feat + extra))],
        [own, node_list.T, expert_ids.T, gate_ints.T, cotangent],
        2 * slots * toks * (toks + feat),
        in_specs=[smem] + [vmem] * 4,
    )
    got = swap_nodes(send)
    (act_grad_parts,) = kernel_call(
        functools.partial(act_grad_body, feat),
        [shape((local, slots, hidden))],
        [got, w_down],
        2 * slots * feat * local * hidden,
    )
    far = lax.all_gather(tokens, "local", axis=0, tiled=False, axis_index_groups=far_groups)
    far, act_grad_parts = lax.optimization_barrier((far, act_grad_parts))
    far = far.reshape(high * toks, feat)
    act_grad = lax.psum_scatter(act_grad_parts, "local", scatter_dimension=0, tiled=False)
    full = lax.all_gather(far, "local", axis=0, tiled=False, axis_index_groups=near_groups)
    full = full.reshape(local, toks, feat)
    (send_rows,) = kernel_call(
        functools.partial(spread_body, order, feat),
        [shape((slots, width))],
        [place, full],
        2 * slots * toks * width,
    )
    rows = swap_nodes(send_rows)
    act, pre_gate, pre_up = kernel_call(
        functools.partial(up_body, feat),
        [shape((slots, hidden)), shape((slots, hidden), F32), shape((slots, hidden), F32)],
        [rows, w_gate, w_up, got],
        4 * slots * width * hidden,
    )
    (grad_parts,) = kernel_call(
        functools.partial(row_grad_body, feat),
        [shape((local, slots, feat))],
        [act_grad, pre_gate, pre_up, got, w_gate, w_up],
        4 * slots * width * hidden,
    )
    row_grad = lax.psum_scatter(grad_parts, "local", scatter_dimension=0, tiled=False)

    far_act = lax.all_gather(act, "local", axis=0, tiled=False, axis_index_groups=far_groups)
    copies = jnp.broadcast_to(far_act[None], (low,) + far_act.shape)
    full_act = lax.all_to_all(
        copies, "local", split_axis=0, concat_axis=0, tiled=True, axis_index_groups=near_groups
    ).reshape(local, slots, hidden)
    (out_rows,) = kernel_call(
        functools.partial(down_body, order),
        [shape((slots, feat))],
        [full_act, w_down],
        2 * slots * feat * local * hidden,
    )
    combine = functools.partial(
        kernel_call, combine_body, [shape((toks, feat))], flops=2 * slots * toks * feat
    )
    (mixed,) = combine([place, swap_nodes(out_rows)])
    (grad_tokens,) = combine([place, swap_nodes(row_grad)])
    return mixed, grad_tokens


def solution(mesh):
    in_specs = (
        P("node", "local"),
        P("node", "local"),
        P("node", None),
        P("node", None),
        P("node", None),
        P(None, ("node", "local")),
        P(None, ("node", "local")),
        P("node", "local"),
    )
    out_specs = (P("node", "local"), P("node", "local"))
    return jax.shard_map(
        per_device, mesh=mesh, in_specs=in_specs, out_specs=out_specs, check_vma=False
    )
```

```python
import functools

import jax
import jax.numpy as jnp
from jax import lax
from jax.experimental import pallas as pl
from jax.experimental.pallas import tpu as pltpu
from jax.sharding import PartitionSpec as P

EXP_NODE = 2
F32 = jnp.float32
BF16 = jnp.bfloat16
NT = (((1,), (1,)), ((), ()))
TN = (((0,), (0,)), ((), ()))
NN = (((1,), (0,)), ((), ()))


def dot(a, b, dims=NN):
    return lax.dot_general(a, b, dims, preferred_element_type=F32)


def kernel_call(body, outs, args, flops, fetch=(), scalars=(), unread=(), vmem_mib=32):
    moved = sum(a.size * a.dtype.itemsize for a in args)
    moved += sum(o.size * o.dtype.itemsize for o in outs)
    vmem = pl.BlockSpec(memory_space=pltpu.VMEM)
    specs = [vmem] * len(args)
    for index in (*fetch, *unread):
        specs[index] = pl.BlockSpec(memory_space=pl.ANY)
    for index in scalars:
        specs[index] = pl.BlockSpec(memory_space=pltpu.SMEM)
    scratch = [pltpu.VMEM(args[index].shape, args[index].dtype) for index in fetch]
    if fetch:
        scratch.append(pltpu.SemaphoreType.DMA((len(fetch),)))

    def whole(*refs):
        refs = list(refs)
        count = len(args) + len(outs)
        copies = []
        for number, index in enumerate(fetch):
            copies.append(
                pltpu.make_async_copy(refs[index], refs[count + number], refs[-1].at[number])
            )
            refs[index] = refs[count + number]
        for copy in copies:
            copy.start()
        for copy in copies:
            copy.wait()
        body(*refs[:count])

    return pl.pallas_call(
        whole,
        out_shape=outs,
        in_specs=specs,
        out_specs=[vmem] * len(outs),
        scratch_shapes=scratch,
        compiler_params=pltpu.CompilerParams(vmem_limit_bytes=vmem_mib * 1024 * 1024),
        cost_estimate=pl.CostEstimate(flops=flops, bytes_accessed=moved, transcendentals=0),
        name=body.func.__name__ if isinstance(body, functools.partial) else body.__name__,
    )(*args)


def shape(dims, dtype=BF16):
    return jax.ShapeDtypeStruct(dims, dtype)


def route_body(cap, own_ref, nodes_ref, experts_ref, counts_ref, cot_ref, place_ref, send_ref):
    slots, toks = place_ref.shape
    feat = cot_ref.shape[1]
    slot = lax.broadcasted_iota(jnp.int32, (slots, toks), 0)
    group = slot // cap
    within = slot - group * cap
    named = jnp.zeros((slots, toks), F32)
    for j in range(nodes_ref.shape[0]):
        named = jnp.where(nodes_ref[j : j + 1, :] == group, 1.0, named)
    before = lax.broadcasted_iota(jnp.int32, (toks, toks), 0)
    after = lax.broadcasted_iota(jnp.int32, (toks, toks), 1)
    earlier = jnp.where(before < after, 1.0, 0.0).astype(BF16)
    rank = dot(named.astype(BF16), earlier)
    place = jnp.where(rank == within.astype(F32), named, 0.0)
    place_ref[...] = place.astype(BF16)
    counts = counts_ref[...].astype(F32)
    share = counts / jnp.sum(counts, axis=0, keepdims=True)
    expert = group * EXP_NODE + own_ref[0]
    picked = jnp.zeros((slots, toks), F32)
    for k in range(experts_ref.shape[0]):
        picked = picked + jnp.where(experts_ref[k : k + 1, :] == expert, share[k : k + 1, :], 0.0)
    gate = jnp.sum(picked * place, axis=1, keepdims=True)
    send_ref[:, :feat] = dot(place.astype(BF16), cot_ref[...]).astype(BF16)
    send_ref[:, feat:] = jnp.broadcast_to(gate, (slots, send_ref.shape[1] - feat)).astype(BF16)


def spread_body(order, feat, place_ref, full_ref, send_ref):
    for index, z in enumerate(order):
        rows = dot(place_ref[...], full_ref[index])
        send_ref[:, z * feat : (z + 1) * feat] = rows.astype(BF16)


def act_grad_body(order, feat, got_ref, down_ref, out_ref):
    hidden = out_ref.shape[2]
    for index, z in enumerate(order):
        rows = slice(z * hidden, (z + 1) * hidden)
        out_ref[index] = dot(got_ref[:, :feat], down_ref[rows, :], NT).astype(BF16)


def near_sum_body(high_ref, parts_ref, *out_refs):
    high = len(out_refs)
    for step in range(high):
        block = lax.rem(high_ref[0] + step, high)
        total = parts_ref[0, block].astype(F32)
        for sender in range(1, parts_ref.shape[0]):
            total = total + parts_ref[sender, block].astype(F32)
        out_refs[step][...] = total.astype(BF16)


def add_body(*refs):
    total = refs[0][...].astype(F32)
    for ref in refs[1:-1]:
        total = total + ref[...].astype(F32)
    refs[-1][...] = total.astype(refs[-1].dtype)


def expert_body(feat, rows_ref, gate_w_ref, up_w_ref, got_ref, grad_ref, act_ref, out_ref):
    pre_gate = dot(rows_ref[...], gate_w_ref[...])
    pre_up = dot(rows_ref[...], up_w_ref[...])
    gate = got_ref[:, feat:].astype(F32)
    sig = jax.nn.sigmoid(pre_gate)
    gated = pre_gate * sig * gate
    act_ref[...] = (gated * pre_up).astype(BF16)
    grad = grad_ref[...]
    grad_up = (grad * gated).astype(BF16)
    grad_pre = (grad * (gate * pre_up * sig * (1.0 + pre_gate * (1.0 - sig)))).astype(BF16)
    for start in range(0, out_ref.shape[1], feat):
        cols = slice(start, start + feat)
        part = dot(grad_pre, gate_w_ref[cols, :], NT) + dot(grad_up, up_w_ref[cols, :], NT)
        out_ref[:, cols] = part.astype(BF16)


def down_body(parts, *refs):
    act_refs, down_ref, out_ref = refs[:parts], refs[-2], refs[-1]
    total = jnp.zeros(out_ref.shape, F32)
    first = 0
    for act_ref in act_refs:
        low, high, _, hidden = act_ref.shape
        for b in range(high):
            for a in range(0, low, 2):
                z = low * (first + b) + a
                act = jnp.concatenate([act_ref[a, b], act_ref[a + 1, b]], axis=1)
                total = total + dot(act, down_ref[z * hidden : (z + 2) * hidden, :])
        first += high
    out_ref[...] = total.astype(BF16)


def combine_body(place_ref, back_ref, out_ref):
    out_ref[...] = dot(place_ref[...], back_ref[...], TN).astype(BF16)


def combine_parts_body(order, feat, place_ref, back_ref, out_ref):
    for index, z in enumerate(order):
        cols = slice(z * feat, (z + 1) * feat)
        out_ref[index] = dot(place_ref[...], back_ref[:, cols], TN).astype(BF16)


def per_device(tokens, cotangent, node_list, expert_ids, gate_ints, w_gate, w_up, w_down):
    toks, feat = tokens.shape
    width, hidden = w_gate.shape
    nodes = lax.axis_size("node")
    local = lax.axis_size("local")
    slots = toks * node_list.shape[1]
    cap = slots // nodes
    low = 4
    high = local // low
    far_groups = [[low * b + a for b in range(high)] for a in range(low)]
    near_groups = [[low * a + b for b in range(low)] for a in range(high)]
    order = [low * b + a for a in range(low) for b in range(high)]
    extra = 128

    def swap_nodes(value):
        cut = value.reshape(nodes, cap, value.shape[1])
        moved = lax.all_to_all(cut, "node", split_axis=0, concat_axis=0, tiled=True)
        return moved.reshape(value.shape)

    own = (lax.axis_index("local") // (local // EXP_NODE)).astype(jnp.int32).reshape(1)
    place, send = kernel_call(
        functools.partial(route_body, cap),
        [shape((slots, toks)), shape((slots, feat + extra))],
        [own, node_list.T, expert_ids.T, gate_ints.T, cotangent],
        2 * slots * toks * (toks + feat),
        fetch=(1, 2, 3, 4),
        scalars=(0,),
        vmem_mib=63,
    )
    got = swap_nodes(send)
    (act_grad_parts,) = kernel_call(
        functools.partial(act_grad_body, order, feat),
        [shape((local, slots, hidden))],
        [got, w_down],
        2 * slots * feat * local * hidden,
    )

    own_high = (lax.axis_index("local") // low).astype(jnp.int32).reshape(1)

    def swap_near(parts):
        count, rows, cols = parts.shape
        moved = lax.all_to_all(
            parts.reshape(low, high * rows, cols),
            "local",
            split_axis=0,
            concat_axis=0,
            tiled=True,
            axis_index_groups=near_groups,
        )
        return kernel_call(
            near_sum_body,
            [shape((rows, cols))] * high,
            [own_high, moved.reshape(low, high, rows, cols)],
            count * rows * cols,
            scalars=(0,),
        )

    def swap_far(sums):
        moved = [sums[0]]
        for step in range(1, high):
            pairs = [(z, (z + step * low) % local) for z in range(local)]
            moved.append(lax.ppermute(sums[step], "local", pairs))
        return moved

    def gather(value, groups):
        return lax.all_gather(value, "local", axis=0, tiled=True, axis_index_groups=groups)

    far = gather(tokens, far_groups)
    far, act_grad_parts = lax.optimization_barrier((far, act_grad_parts))
    act_grads = swap_far(swap_near(act_grad_parts))
    (act_grad,) = kernel_call(
        add_body, [shape((slots, hidden), F32)], act_grads, high * slots * hidden
    )
    full = gather(far, near_groups).reshape(local, toks, feat)
    (send_rows,) = kernel_call(
        functools.partial(spread_body, order, feat),
        [shape((slots, width))],
        [place, full],
        2 * slots * toks * width,
    )
    rows = swap_nodes(send_rows)
    act, grad_parts = kernel_call(
        functools.partial(expert_body, feat),
        [shape((slots, hidden)), shape((slots, width))],
        [rows, w_gate, w_up, got, act_grad],
        8 * slots * width * hidden,
    )

    far_act = gather(act, far_groups)
    first_act, last_act = far_act[: high // 2 * slots], far_act[high // 2 * slots :]
    first_act = gather(first_act, near_groups)
    back_parts = swap_nodes(grad_parts)
    first_act, back_parts = lax.optimization_barrier((first_act, back_parts))
    (own_parts,) = kernel_call(
        functools.partial(combine_parts_body, order, feat),
        [shape((local, toks, feat))],
        [place, back_parts],
        2 * slots * toks * width,
    )
    last_act, own_parts = lax.optimization_barrier((last_act, own_parts))
    near_sums = swap_near(own_parts)
    last_act = gather(last_act, near_groups)
    (out_rows,) = kernel_call(
        functools.partial(down_body, 2),
        [shape((slots, feat))],
        [part.reshape(low, high // 2, slots, hidden) for part in (first_act, last_act)] + [w_down],
        2 * slots * feat * local * hidden,
    )
    near_sums, out_rows = lax.optimization_barrier((near_sums, out_rows))
    far_sums = swap_far(near_sums)
    (mixed,) = kernel_call(
        combine_body, [shape((toks, feat))], [place, swap_nodes(out_rows)], 2 * slots * toks * feat
    )
    (grad_tokens,) = kernel_call(
        add_body, [shape((toks, feat))], far_sums, high * toks * feat
    )
    return mixed, grad_tokens


def solution(mesh):
    in_specs = (
        P("node", "local"),
        P("node", "local"),
        P("node", None),
        P("node", None),
        P("node", None),
        P(None, ("node", "local")),
        P(None, ("node", "local")),
        P("node", "local"),
    )
    out_specs = (P("node", "local"), P("node", "local"))
    return jax.shard_map(
        per_device, mesh=mesh, in_specs=in_specs, out_specs=out_specs, check_vma=False
    )
```
